256 devices in a mesh: shot: 32 (over z, y_hi, core), surf: 8 (over y_lo, x).
Axes of the slice: x: 4, y: 4 (y_hi: 2, y_lo: 2; y = y_hi * 2 + y_lo), z: 8, core: 2. Of those that a mesh axis runs over, the one named last changes fastest.
Arguments:
- shot_data: float32 [2, 2, 6144, 2048], P(None, None, 'shot', 'surf'), may hold values from -6 to 6
- surface_data: float32 [2, 2, 2048, 4096], P(None, None, 'surf', 'shot'), may hold values from -0.1875 to 0.1875
Outputs:
- multiples: float32 [2, 2, 6144, 4096], P(None, None, 'shot', 'surf')
The draws below stay inside these ranges and needn't reach their ends.
All inputs are finite; a program needn't handle non-finite values.
Results may differ from the reference program's by a relative error of at most 0.0001.
Values sent between devices are 32-bit elements; how exact they have to be, the bound alone decides.
No kernel may reach another device: no remote copies, remote signals or barrier semaphores. Data moves between devices by JAX's collectives and lax.ppermute only.
A program may use at most 128 MiB of HBM per device.

```python
import jax
import jax.numpy as jnp
from jax import lax

FREQS = 2
K = 2048
R = 4096
S = 6144


def with_spikes(array, own_key, source, target, parts, factor):
    owner, partner = [(jnp.arange(array.shape[axis_at]) // (array.shape[axis_at] // parts)).reshape([-1 if axis == axis_at else 1 for axis in range(array.ndim)]) for axis_at in (source, target)]
    chosen = jax.random.permutation(own_key, parts)[partner]
    strong = (owner == chosen) | (owner == (partner + parts // 2) % parts)
    return jnp.where(strong, factor * array, array)


def steps_of(rng, extent, shards, smallest, largest):
    def one(position, parts):
        heights = jax.random.uniform(jax.random.fold_in(jax.random.fold_in(rng, 6), position), (parts,), jnp.float32, smallest / len(shards), largest / len(shards))
        return jnp.repeat(jnp.exp(heights), extent[position] // parts).reshape((-1,) + (1,) * (len(extent) - position - 1))

    loudness = one(*shards[0])
    for cut in shards[1:]:
        loudness = loudness * one(*cut)
    return loudness


def bell_draw(stream_key, shape, deviation, reach, shards=(), held_as=jnp.bfloat16):
    values = deviation * jax.random.normal(stream_key, shape, jnp.float32)
    if shards:
        values = values * steps_of(stream_key, shape, shards, -0.22, 0.18)
    return jnp.clip(values, -reach, reach).astype(held_as)


def heavy_noise(stream_key, shape, spread, reach, pieces, heavy, held_as=jnp.bfloat16):
    drawn = spread * jax.random.normal(stream_key, shape, jnp.float32)
    if pieces:
        drawn = drawn * steps_of(stream_key, shape, pieces, -0.22, 0.18)
    return jnp.clip(with_spikes(drawn, jax.random.fold_in(stream_key, 3), *heavy), -reach, reach).astype(held_as)


def setup_inputs(seed: int = 0) -> dict:
    splits = jax.random.split(jax.random.key(seed), 3)
    shot_data = bell_draw(splits[0], (FREQS, 2, S, K), 1.0, 6.0, ((2, 32), (3, 8)), jnp.float32)
    surface_data = heavy_noise(splits[1], (FREQS, 2, K, R), (2 * K) ** -0.5, 0.1875, ((2, 8), (3, 32)), (2, 3, 32, 2.75), jnp.float32)
    return dict(shot_data=shot_data, surface_data=surface_data)


def reference(shot_data, surface_data):
    highest = lax.Precision.HIGHEST
    slices = []
    for frequency in range(FREQS):
        real_left = shot_data[frequency, 0]
        imag_left = shot_data[frequency, 1]
        real_right = surface_data[frequency, 0]
        imag_right = surface_data[frequency, 1]
        real_out = jnp.dot(real_left, real_right, precision=highest, preferred_element_type=jnp.float32) - jnp.dot(imag_left, imag_right, precision=highest, preferred_element_type=jnp.float32)
        imag_out = jnp.dot(real_left, imag_right, precision=highest, preferred_element_type=jnp.float32) + jnp.dot(imag_left, real_right, precision=highest, preferred_element_type=jnp.float32)
        slices.append(jnp.stack([real_out, imag_out]))
    return jnp.stack(slices)
```

```python
import functools

import jax
import jax.numpy as jnp
from jax import lax
from jax.experimental import pallas as pl
from jax.experimental.pallas import tpu as pltpu
from jax.sharding import PartitionSpec as P

AXES = ("shot", "surf")
NX, NZ = 4, 8


def device_id(x, y_lo, y_hi, z, core):
    return ((z * 2 + y_hi) * 2 + core) * (2 * NX) + y_lo * NX + x


def coordinates():
    return [
        (x, y_lo, y_hi, z, core)
        for x in range(NX)
        for y_lo in range(2)
        for y_hi in range(2)
        for z in range(NZ)
        for core in range(2)
    ]


def move(array, where):
    pairs = [(device_id(*at), device_id(*where(*at))) for at in coordinates()]
    return lax.ppermute(array, AXES, pairs)


def along_z(array, step):
    return move(array, lambda x, yl, yh, z, c: (x, yl, yh, (z + step) % NZ, c))


def along_x(array, step):
    return move(array, lambda x, yl, yh, z, c: ((x + step) % NX, yl, yh, z, c))


def flip_y(array, lo, hi):
    return move(array, lambda x, yl, yh, z, c: (x, yl ^ lo, yh ^ hi, z, c))


def swap_cores(array):
    return move(array, lambda x, yl, yh, z, c: (x, yl, yh, z, c ^ 1))


def home_z(z, y_hi, core):
    return (z % NX - 1 + core + 2 * (z // NX) + 4 * y_hi) % NZ


def spread(piece, freq_of_x):
    return move(
        piece, lambda x, yl, yh, z, c: (z % NX, yl, freq_of_x(x), home_z(z, yh, c), x // 2)
    )


def split_kernel(place, *refs):
    *blocks, high_ref, low_ref = refs
    rows, depth = blocks[0].shape[1:]
    for half in range(2):
        for step in range(NX):
            for part in range(2):
                value = blocks[half * NX + step][part]
                high = value.astype(jnp.bfloat16)
                low = (value - high.astype(jnp.float32)).astype(jnp.bfloat16)
                at = pl.ds(pl.multiple_of(place[step] * (2 * depth) + part * depth, depth), depth)
                high_ref[half * rows : (half + 1) * rows, at] = high
                low_ref[half * rows : (half + 1) * rows, at] = low


def split_shots(place, blocks):
    rows, depth = blocks[0].shape[1:]
    out = jax.ShapeDtypeStruct((2 * rows, NX * 2 * depth), jnp.bfloat16)
    return pl.pallas_call(
        split_kernel,
        out_shape=(out, out),
        in_specs=[pl.BlockSpec(memory_space=pltpu.SMEM)]
        + [pl.BlockSpec(memory_space=pltpu.VMEM)] * len(blocks),
        out_specs=(pl.BlockSpec(memory_space=pltpu.VMEM),) * 2,
        compiler_params=pltpu.CompilerParams(vmem_limit_bytes=32 * 1024 * 1024),
        cost_estimate=pl.CostEstimate(flops=0, bytes_accessed=rows * depth * 128, transcendentals=0),
        name="split_shots",
    )(place, *blocks)


def product_kernel(flag, high_ref, low_ref, *refs):
    pieces = refs[:4]
    own, over_hi, over_lo, over_both, w_high, w_low = refs[4:]
    depth, columns = pieces[0].shape[2:]
    rows = own.shape[1]
    second = flag[0] == 1
    for side in range(2):
        for position in range(NX):
            core, slot = position // 2, position % 2
            first_group, second_group = pieces[core], pieces[2 + core]
            if side:
                first_group, second_group = second_group, first_group
            real = jnp.where(second, second_group[slot, 0], first_group[slot, 0])
            imag = jnp.where(second, second_group[slot, 1], first_group[slot, 1])
            real_high, imag_high = real.astype(jnp.bfloat16), imag.astype(jnp.bfloat16)
            real_low = (real - real_high.astype(jnp.float32)).astype(jnp.bfloat16)
            imag_low = (imag - imag_high.astype(jnp.float32)).astype(jnp.bfloat16)
            for to, r, i in ((w_high, real_high, imag_high), (w_low, real_low, imag_low)):
                base = position * 2 * depth
                to[side, base : base + depth, :columns] = r
                to[side, base : base + depth, columns:] = i
                to[side, base + depth : base + 2 * depth, :columns] = -i
                to[side, base + depth : base + 2 * depth, columns:] = r
        dot = functools.partial(jnp.dot, preferred_element_type=jnp.float32)
        total = (
            dot(high_ref[...], w_low[side]) + dot(low_ref[...], w_high[side])
        ) + dot(high_ref[...], w_high[side])
        near, far = (over_lo, over_both) if side else (own, over_hi)
        near[0], near[1] = total[:rows, :columns], total[:rows, columns:]
        far[0], far[1] = total[rows:, :columns], total[rows:, columns:]


def products(flag, high, low, pieces):
    rows = high.shape[0] // 2
    _, _, depth, columns = pieces[0].shape
    out = jax.ShapeDtypeStruct((2, rows, columns), jnp.float32)
    weights = pltpu.VMEM((2, NX * 2 * depth, 2 * columns), jnp.bfloat16)
    flops = 2 * 3 * high.shape[0] * high.shape[1] * 4 * columns
    return pl.pallas_call(
        product_kernel,
        out_shape=(out,) * 4,
        in_specs=[pl.BlockSpec(memory_space=pltpu.SMEM)]
        + [pl.BlockSpec(memory_space=pltpu.VMEM)] * 6,
        out_specs=(pl.BlockSpec(memory_space=pltpu.VMEM),) * 4,
        scratch_shapes=[weights, weights],
        compiler_params=pltpu.CompilerParams(vmem_limit_bytes=40 * 1024 * 1024),
        cost_estimate=pl.CostEstimate(flops=flops, bytes_accessed=7 << 20, transcendentals=0),
        name="products",
    )(flag, high, low, *pieces)


def finish_kernel(table, *refs):
    *parts, out_ref = refs
    columns = parts[0].shape[2]
    mine = table[0]
    for batch in range(len(parts) // 4):
        own, from_lo, from_hi, from_both = parts[4 * batch : 4 * batch + 4]
        at = pl.ds(pl.multiple_of(table[1 + batch] * columns, columns), columns)
        for part in range(2):
            out_ref[mine, part, :, at] = own[part] + from_lo[part]
            out_ref[1 - mine, part, :, at] = from_hi[part] + from_both[part]


def finish(table, parts):
    _, rows, columns = parts[0].shape
    shape = (2, 2, rows, columns * len(parts) // 4)
    return pl.pallas_call(
        finish_kernel,
        out_shape=jax.ShapeDtypeStruct(shape, jnp.float32),
        in_specs=[pl.BlockSpec(memory_space=pltpu.SMEM)]
        + [pl.BlockSpec(memory_space=pltpu.VMEM)] * len(parts),
        out_specs=pl.BlockSpec(memory_space=pltpu.VMEM),
        compiler_params=pltpu.CompilerParams(vmem_limit_bytes=32 * 1024 * 1024),
        cost_estimate=pl.CostEstimate(flops=0, bytes_accessed=5 << 20, transcendentals=0),
        name="finish",
    )(table, *parts)


def on_device(shot_data, surface_data):
    shot, surf = lax.axis_index("shot"), lax.axis_index("surf")
    z, y_hi, core = shot // 4, (shot // 2) % 2, shot % 2
    y_lo, x = surf // NX, surf % NX

    even = x % 2
    slot0 = spread(lax.dynamic_index_in_dim(surface_data, even, keepdims=False), lambda x: x % 2)
    slot1 = spread(lax.dynamic_index_in_dim(surface_data, 1 - even, keepdims=False), lambda x: 1 - x % 2)
    here = jnp.stack([slot0, slot1])

    mine = lax.dynamic_index_in_dim(shot_data, y_hi, keepdims=False)
    theirs = flip_y(lax.dynamic_index_in_dim(shot_data, 1 - y_hi, keepdims=False), 0, 1)
    blocks = [mine] + [along_x(mine, step) for step in range(1, NX)]
    blocks += [theirs] + [along_x(theirs, step) for step in range(1, NX)]
    sources = [(x - step) % NX for step in range(NX)]
    place = jnp.stack([2 * ((s // 2) ^ core) + ((s % 2) ^ y_hi) for s in sources]).astype(jnp.int32)
    high, low = split_shots(place, blocks)

    held = {0: here}
    up = down = here
    for step in range(1, NZ // 2):
        up, down = along_z(up, 1), along_z(down, -1)
        held[-step], held[step] = up, down
    held[NZ // 2] = jnp.stack([along_z(up[0], 1), along_z(down[1], -1)])
    both = {distance: (piece, swap_cores(piece)) for distance, piece in held.items()}

    parts, table = [], [y_hi]
    for one, two in ((-1, 1), (0, 2), (-3, 3), (-2, 4)):
        ranks = [(z + distance - x + 1) % NZ for distance in (one, two)]
        sides = [(rank // 2) % 2 for rank in ranks]
        flag = (sides[0] != y_lo).astype(jnp.int32)
        own, over_hi, over_lo, over_both = products(flag[None], high, low, both[one] + both[two])
        parts += [own, flip_y(over_lo, 1, 0), flip_y(over_hi, 0, 1), flip_y(over_both, 1, 1)]
        rank = jnp.where(flag == 1, ranks[1], ranks[0])
        table.append(rank % 2 + 2 * (rank // 4))
    return finish(jnp.stack(table).astype(jnp.int32), parts)


def solution(mesh):
    return jax.shard_map(
        on_device,
        mesh=mesh,
        in_specs=(P(None, None, "shot", "surf"), P(None, None, "surf", "shot")),
        out_specs=P(None, None, "shot", "surf"),
        check_vma=False,
    )
```

```python
import functools

import jax
import jax.numpy as jnp
from jax import lax
from jax.experimental import pallas as pl
from jax.experimental.pallas import tpu as pltpu
from jax.sharding import PartitionSpec as P

AXES = ("shot", "surf")
NX, NZ = 4, 8
POINT_BLOCKS = 2 * NX


def device_id(x, y_lo, y_hi, z, core):
    return ((z * 2 + y_hi) * 2 + core) * (2 * NX) + y_lo * NX + x


def move(array, where):
    pairs = [
        (device_id(x, yl, yh, z, c), device_id(*where(x, yl, yh, z, c)))
        for x in range(NX)
        for yl in range(2)
        for yh in range(2)
        for z in range(NZ)
        for c in range(2)
    ]
    return lax.ppermute(array, AXES, pairs)


def along_x(array, step):
    return move(array, lambda x, yl, yh, z, c: ((x + step) % NX, yl, yh, z, c))


def flip_y(array, lo, hi):
    return move(array, lambda x, yl, yh, z, c: (x, yl ^ lo, yh ^ hi, z, c))


def spread(piece, number):
    freq, half = number // 2, number % 2
    return move(piece, lambda x, yl, yh, z, c: (yh + 2 * c, half ^ yl, freq ^ (x % 2), z, x // 2))


def gather_z(array):
    groups = [
        [device_id(x, yl, yh, z, c) for z in range(NZ) for c in range(2)]
        for yh in range(2)
        for yl in range(2)
        for x in range(NX)
    ]
    return lax.all_gather(array, AXES, axis_index_groups=groups, axis=0, tiled=True)


def exchange(array):
    groups = [
        [device_id(x, yl, yh, z, c) for yh in range(2) for yl in range(2) for x in range(NX)]
        for z in range(NZ)
        for c in range(2)
    ]
    return lax.all_to_all(array, AXES, 0, 0, axis_index_groups=groups, tiled=True)


def together(*arrays):
    return lax.optimization_barrier(arrays)


VMEM = pl.BlockSpec(memory_space=pltpu.VMEM)
ANY = pl.BlockSpec(memory_space=pl.ANY)


def place():
    surf, shot = lax.axis_index("surf"), lax.axis_index("shot")
    return lax.rem(surf, NX), lax.div(surf, NX), lax.rem(lax.div(shot, 2), 2)


def turned(value):
    return pltpu.roll(value, value.shape[1] // 2, 1)


def left(shape):
    return lax.broadcasted_iota(jnp.int32, shape, 1) < shape[1] // 2


def parts_of(value):
    high = value.astype(jnp.bfloat16)
    return high, (value - high.astype(jnp.float32)).astype(jnp.bfloat16)


def pack_kernel(surface, *pieces):
    x, y_lo, _ = place()
    for number in range(2):
        freq = number ^ lax.rem(x, 2)
        real, imag = surface[freq, 0], surface[freq, 1]
        first = jnp.where(left(real.shape), real, turned(imag))
        second = jnp.where(left(real.shape), turned(real), imag)
        pieces[2 * number][...] = jnp.where(y_lo == 0, first, second)
        pieces[2 * number + 1][...] = jnp.where(y_lo == 0, second, first)


def pack(surface_data):
    out = jax.ShapeDtypeStruct(surface_data.shape[2:], jnp.float32)
    return pl.pallas_call(
        pack_kernel,
        out_shape=(out,) * 4,
        in_specs=[VMEM],
        out_specs=(VMEM,) * 4,
        cost_estimate=pl.CostEstimate(flops=0, bytes_accessed=1 << 20, transcendentals=0),
        name="pack",
    )(surface_data)


def split_kernel(*refs):
    *blocks, high_ref, low_ref, held, arrived = refs
    _, _, _, rows, depth = held.shape
    copies = [
        pltpu.make_async_copy(block, held.at[number], arrived.at[number])
        for number, block in enumerate(blocks)
    ]
    for copy in copies:
        copy.start()
    for number, copy in enumerate(copies):
        copy.wait()
        for half in range(2):
            for part in range(2):
                first = (2 * part + half) * rows
                at = slice(first, first + rows), slice(number * depth, (number + 1) * depth)
                high_ref[at], low_ref[at] = parts_of(held[number, half, part])


def split_shots(blocks):
    _, _, rows, depth = blocks[0].shape
    out = jax.ShapeDtypeStruct((4 * rows, POINT_BLOCKS * depth), jnp.bfloat16)
    return pl.pallas_call(
        split_kernel,
        out_shape=(out, out),
        in_specs=[ANY] * len(blocks),
        out_specs=(VMEM,) * 2,
        scratch_shapes=[
            pltpu.VMEM((len(blocks), *blocks[0].shape), jnp.float32),
            pltpu.SemaphoreType.DMA((len(blocks),)),
        ],
        compiler_params=pltpu.CompilerParams(vmem_limit_bytes=12 * 1024 * 1024),
        cost_estimate=pl.CostEstimate(flops=0, bytes_accessed=12 << 20, transcendentals=0),
        name="split_shots",
    )(*blocks)


def product_kernel(gathered, high_ref, low_ref, out, w_high, w_low):
    rows = out.shape[1]
    points, columns = gathered.shape[1:]
    x, y_lo, y_hi = place()
    dot = functools.partial(jnp.dot, preferred_element_type=jnp.float32)
    for pair in range(NZ // 2):
        for side in range(2):
            for number in range(POINT_BLOCKS):
                across, step = number // NX, number % NX
                source = lax.rem(x + (NX - step), NX)
                freq = lax.rem(source, 2) ^ y_hi
                piece = (2 * pair + side) * 8 + lax.div(source, 2) * 4 + freq * 2 + across
                at = (
                    pair,
                    slice(number * points, (number + 1) * points),
                    slice(side * columns, (side + 1) * columns),
                )
                w_high[at], w_low[at] = parts_of(gathered[piece])
        total = (
            dot(high_ref[...], w_low[pair]) + dot(low_ref[...], w_high[pair])
        ) + dot(high_ref[...], w_high[pair])
        for side in range(2):
            at = slice(side * columns, (side + 1) * columns)
            real, imag = total[: 2 * rows, at], turned(total[2 * rows :, at])
            value = real + jnp.where(left(imag.shape), -imag, imag)
            out[y_hi * NZ + 2 * pair + side] = value[:rows]
            out[(1 - y_hi) * NZ + 2 * pair + side] = value[rows:]


def products(gathered, high, low):
    rows, depth = high.shape[0] // 4, high.shape[1]
    _, points, columns = gathered.shape
    flops = 2 * 3 * 4 * rows * depth * columns * NZ
    weights = pltpu.VMEM((NZ // 2, depth, 2 * columns), jnp.bfloat16)
    return pl.pallas_call(
        product_kernel,
        out_shape=jax.ShapeDtypeStruct((2 * NZ, rows, columns), jnp.float32),
        in_specs=[VMEM, VMEM, VMEM],
        out_specs=VMEM,
        scratch_shapes=[weights, weights],
        compiler_params=pltpu.CompilerParams(vmem_limit_bytes=30 * 1024 * 1024),
        cost_estimate=pl.CostEstimate(flops=flops, bytes_accessed=15 << 20, transcendentals=0),
        name="products",
    )(gathered, high, low)


def finish_kernel(came, out):
    columns = came.shape[2]
    for freq in range(2):
        for x in range(NX):
            first, second = came[freq * NZ + x], came[freq * NZ + NX + x]
            shard = 2 * (x % 2) + x // 2
            to = slice(shard * columns, (shard + 1) * columns)
            out[freq, 0, :, to] = jnp.where(left(first.shape), first, turned(second))
            out[freq, 1, :, to] = jnp.where(left(first.shape), turned(first), second)


def finish(came):
    _, rows, columns = came.shape
    return pl.pallas_call(
        finish_kernel,
        out_shape=jax.ShapeDtypeStruct((2, 2, rows, columns * NX), jnp.float32),
        in_specs=[VMEM],
        out_specs=VMEM,
        compiler_params=pltpu.CompilerParams(vmem_limit_bytes=16 * 1024 * 1024),
        cost_estimate=pl.CostEstimate(flops=0, bytes_accessed=3 << 20, transcendentals=0),
        name="finish",
    )(came)


def on_device(shot_data, surface_data):
    y_hi = (lax.axis_index("shot") // 2) % 2
    pieces = [spread(piece, number) for number, piece in enumerate(pack(surface_data))]
    mine = lax.dynamic_index_in_dim(shot_data, y_hi, keepdims=False)
    theirs = lax.dynamic_index_in_dim(shot_data, 1 - y_hi, keepdims=False)
    here, theirs = together(jnp.stack(pieces), flip_y(theirs, 0, 1))
    gathered = gather_z(here)

    block = jnp.stack([mine, theirs])
    across, up, down = together(flip_y(block, 1, 0), along_x(block, 1), along_x(block, -1))
    across_up, across_down, up = together(along_x(across, 1), along_x(across, -1), up)
    far, across_far = along_x(up, 1), along_x(across_down, -1)
    high, low = split_shots([block, up, far, down, across, across_up, across_far, across_down])
    return finish(exchange(products(gathered, high, low)))


def solution(mesh):
    return jax.shard_map(
        on_device,
        mesh=mesh,
        in_specs=(P(None, None, "shot", "surf"), P(None, None, "surf", "shot")),
        out_specs=P(None, None, "shot", "surf"),
        check_vma=False,
    )
```
